256 devices in a mesh: fsdp: 32 (over z, x), tp: 8 (over y, core).
Axes of the slice: x: 4, y: 4, z: 8, core: 2. Of those that a mesh axis runs over, the one named last changes fastest.
Arguments:
- grads: bfloat16 [2, 16384, 3, 2048], P(None, 'fsdp', None, 'tp'), may hold values from -60 to 60
- accum: float32 [2, 16384, 3, 2048], P(None, 'fsdp', None, 'tp'), may hold values from 0.1 to 4
- roots: bfloat16 [2, 3, 2048, 2048], P(None, None, 'fsdp', 'tp'), may hold values from -3 to 3
Outputs:
- statistic: float32 [2, 3, 2048, 2048], P(None, None, 'fsdp', 'tp')
- step: float32 [2, 16384, 3, 2048], P(None, 'fsdp', None, 'tp')
The draws below stay inside these ranges and needn't reach their ends.
All inputs are finite; a program needn't handle non-finite values.
Results may differ from the reference program's by a relative error of at most 0.00045.
Values may be sent and summed in bfloat16 or wider, within the bound.
No kernel may reach another device: no remote copies, remote signals or barrier semaphores. Data moves between devices by JAX's collectives and lax.ppermute only.
A program may use at most 128 MiB of HBM per device.

```python
import math
import jax
import jax.numpy as jnp
from jax import lax

FF = 16384
BS = 2048
E = 2
CB = 3


def draw_grads(key, part):
    key = jax.random.fold_in(key, 11)
    noise_key, row_key, col_key = jax.random.split(key, 3)
    shape = (E, FF, CB, BS)
    values = jax.random.truncated_normal(noise_key, -4.0, 4.0, shape, jnp.float32)
    rising = jnp.exp(math.log(3.0) * jnp.arange(FF, dtype=jnp.float32) / FF)
    row_factor = jnp.exp(jax.random.uniform(row_key, (E, FF, 1, 1), jnp.float32) * math.log(10.0)) * rising[None, :, None, None]
    col_factor = jnp.exp(jax.random.uniform(col_key, (E, 1, CB, BS), jnp.float32) * math.log(10.0))
    return (0.05 * values * row_factor * col_factor).astype(jnp.bfloat16)


def draw_roots(key, part):
    key = jax.random.fold_in(key, 23)
    diag_key, noise_key = jax.random.split(key)
    diagonal = jnp.exp(jax.random.uniform(diag_key, (E, CB, 1, BS), jnp.float32, math.log(0.5), math.log(2.0)))
    identity = (jnp.arange(BS)[:, None] == jnp.arange(BS)[None, :]).astype(jnp.float32)
    noise = jax.random.truncated_normal(noise_key, -4.0, 4.0, (E, CB, BS, BS), jnp.float32)
    values = identity[None, None] * diagonal + 0.7 * noise / math.sqrt(BS)
    return values.astype(jnp.bfloat16)


def block_scale(own_key, extent, pieces, least, top_value):
    level = 1.0
    for position, shards_of in pieces:
        steps = jax.random.uniform(jax.random.fold_in(jax.random.fold_in(own_key, 6), position), (shards_of,), jnp.float32, least / len(pieces), top_value / len(pieces))
        level = level * jnp.repeat(jnp.exp(steps), extent[position] // shards_of).reshape((-1,) + (1,) * (len(extent) - 1 - position))
    return level


def setup_inputs(seed: int = 0) -> dict:
    seeds = jax.random.split(jax.random.key(seed), 4)
    grads = draw_grads(jax.random.fold_in(seeds[3], 71), 0)
    accum = jnp.clip(jnp.exp(math.log(4.0) - 3.6888794 * jax.random.uniform(seeds[1], (E, FF, CB, BS), jnp.float32) ** block_scale(seeds[1], (E, FF, CB, BS), ((1, 32), (3, 8)), -0.2, 0.2)), 0.1, 4.0)
    roots = draw_roots(jax.random.fold_in(seeds[3], 71), 0)
    return dict(grads=grads, accum=accum, roots=roots)


EPS = 1e-08

def reference(grads, accum, roots):
    gradient = grads.astype(jnp.float32)

    def per_expert(pair):
        expert_grad, expert_root = pair
        gram_block = jnp.einsum('rjk,rjc->jkc', expert_grad, expert_grad, precision=lax.Precision.HIGHEST) / FF
        direction = jnp.einsum('rjk,jkc->rjc', expert_grad, expert_root.astype(jnp.float32), precision=lax.Precision.HIGHEST)
        return (gram_block, direction)
    statistic, direction = lax.map(per_expert, (gradient, roots))
    adagrad = gradient / (jnp.sqrt(accum + gradient * gradient) + EPS)
    adagrad_sq = lax.optimization_barrier(jnp.sum(adagrad * adagrad, axis=(1, 3)))
    direction_sq = lax.optimization_barrier(jnp.sum(direction * direction, axis=(1, 3)))
    graft_scale = jnp.sqrt(adagrad_sq) / jnp.sqrt(direction_sq + 1e-06)
    step = direction * graft_scale[:, None, :, None]
    return (statistic, step)
```

```python
import jax
import jax.numpy as jnp
from jax import lax
from jax.experimental import pallas as pl
from jax.experimental.pallas import tpu as pltpu
from jax.sharding import PartitionSpec as P

EPS = 1e-08
NZ, NX, NY, NC = 8, 4, 4, 2
AXES = ("fsdp", "tp")
F32 = jnp.float32
F16 = jnp.float16


def shift_x(value, by):
    pairs = [(z * NX + x, z * NX + (x + by) % NX) for z in range(NZ) for x in range(NX)]
    return lax.ppermute(value, "fsdp", pairs)


def shift_y(value, by):
    pairs = [(y * NC + c, (y + by) % NY * NC + c) for y in range(NY) for c in range(NC)]
    return lax.ppermute(value, "tp", pairs)


def swap_cores(value):
    return lax.ppermute(value, "tp", [(i, i ^ 1) for i in range(NY * NC)])


def device(z, x, y, c):
    return ((z * NX + x) * NY + y) * NC + c


GROUPS_XC = [
    [device(z, x, y, c) for x in range(NX) for c in range(NC)] for z in range(NZ) for y in range(NY)
]
GROUPS_ZC = [
    [device(z, x, y, c) for z in range(NZ) for c in range(NC)] for x in range(NX) for y in range(NY)
]
GROUPS_Z = [[z * NX + x for z in range(NZ)] for x in range(NX)]


def spread(value, axis):
    copies = jnp.broadcast_to(value[None], (lax.axis_size(axis),) + value.shape)
    return lax.all_to_all(copies, axis, 0, 0)


def halves(value):
    half = value.shape[0] // 2
    return value[:half], value[half:]


def reduce_x(parts, scale):
    first, second = halves(parts[2] * scale)
    right = shift_x(first.astype(F16), 1)
    left = shift_x(second.astype(F16), -1)
    first, second = halves(parts[1] * scale)
    to_right = jnp.concatenate([first + right.astype(F32), second])
    first, second = halves(parts[3] * scale)
    to_left = jnp.concatenate([first, second + left.astype(F32)])
    right = shift_x(to_right.astype(F16), 1)
    left = shift_x(to_left.astype(F16), -1)
    return parts[0] * scale + right.astype(F32) + left.astype(F32)


def contract_rows(a, b):
    return lax.dot_general(a, b, (((0,), (0,)), ((), ())), preferred_element_type=F32)


def gram_kernel(place, own, before, after, far_up, far_down, cols, out):
    xi, yi = place[0], place[1]
    half = far_up.shape[0]
    rows = out.shape[2]

    def store(part, dy):
        y = lax.rem(yi + dy, NY)
        for i in range(2):
            for x in range(NX):
                start = (i * NX + x) * rows
                out[lax.rem(x - xi + NX, NX), 2 * y + i] = part[start : start + rows]

    store(contract_rows(own[...], cols[...]), 0)
    store(contract_rows(before[...], cols[...]), NY - 1)
    store(contract_rows(after[...], cols[...]), 1)
    store(contract_rows(far_up[...], cols[:half]) + contract_rows(far_down[...], cols[half:]), 2)


def gram_parts(place, pieces):
    own = pieces[0]
    local_rows, wide = own.shape
    rows = wide * NY // (NZ * NX)
    split = 2
    whole = [pl.BlockSpec(piece.shape, lambda i, s: (0, 0)) for piece in pieces]
    return pl.pallas_call(
        gram_kernel,
        grid_spec=pltpu.PrefetchScalarGridSpec(
            num_scalar_prefetch=1,
            grid=(split,),
            in_specs=whole + [pl.BlockSpec((local_rows, wide // split), lambda i, s: (0, i))],
            out_specs=pl.BlockSpec((NX, NZ, rows, wide // split), lambda i, s: (0, 0, 0, i)),
        ),
        out_shape=jax.ShapeDtypeStruct((NX, NZ, rows, wide), F32),
        compiler_params=pltpu.CompilerParams(vmem_limit_bytes=32 << 20),
        cost_estimate=pl.CostEstimate(
            flops=2 * local_rows * wide * wide * NY,
            bytes_accessed=2 * local_rows * wide * NY + 4 * wide * wide * NY,
            transcendentals=0,
        ),
    )(place, *pieces, own)


def direction_kernel(place, own, before, after, far_up, far_down, pieces, mine, theirs, squares, root):
    yi, ci = place[1], place[2]
    rows, slab = pieces.shape[3:]
    half, wide = far_up.shape
    for z in range(NZ):
        for x in range(NX):
            for c in range(NC):
                start = (z * NX + x) * rows
                root[start : start + rows, c * slab : (c + 1) * slab] = pieces[z, x * NC + c, 0]

    def at(dy):
        start = lax.rem(yi + dy, NY) * wide
        return root[pl.ds(pl.multiple_of(start, wide), wide), :]

    def product(a, b):
        return jnp.dot(a, b, preferred_element_type=F32)

    value = product(own[...], at(0)) + product(before[...], at(NY - 1)) + product(after[...], at(1))
    far = at(2)
    for index, piece in enumerate((far_up, far_down)):
        span = slice(index * half, (index + 1) * half)
        part = value[span] + product(piece[...], far)
        first, second = part[:, :slab], part[:, slab:]
        mine[span] = jnp.where(ci == 0, first, second)
        theirs[span] = jnp.where(ci == 0, second, first)
        total = jnp.full((8, 128), jnp.sum(part * part), F32)
        squares[index] = total


def direction_of(place, pieces, roots, block):
    local_rows, wide = pieces[0].shape
    rows, slab = roots.shape[3:]
    result = jax.ShapeDtypeStruct((local_rows, slab), F32)
    specs = [pl.BlockSpec(piece.shape, lambda i, s: (0, 0)) for piece in pieces]
    return pl.pallas_call(
        direction_kernel,
        grid_spec=pltpu.PrefetchScalarGridSpec(
            num_scalar_prefetch=1,
            grid=(1,),
            in_specs=specs
            + [pl.BlockSpec((NZ, NX * NC, 1, rows, slab), lambda i, s: (0, 0, block, 0, 0))],
            out_specs=[
                pl.BlockSpec((local_rows, slab), lambda i, s: (0, 0)),
                pl.BlockSpec((local_rows, slab), lambda i, s: (0, 0)),
                pl.BlockSpec((2, 8, 128), lambda i, s: (0, 0, 0)),
            ],
            scratch_shapes=[pltpu.VMEM((wide * NY, wide), jnp.bfloat16)],
        ),
        out_shape=[result, result, jax.ShapeDtypeStruct((2, 8, 128), F32)],
        compiler_params=pltpu.CompilerParams(vmem_limit_bytes=32 << 20),
        cost_estimate=pl.CostEstimate(
            flops=2 * local_rows * wide * wide * NY,
            bytes_accessed=2 * (local_rows + wide) * wide * NY + 4 * local_rows * wide,
            transcendentals=0,
        ),
    )(place, *pieces, roots)


def on_device(grads, accum, roots):
    experts, local_rows, blocks, slab = grads.shape
    fsdp, tp = lax.axis_index("fsdp"), lax.axis_index("tp")
    core = lax.rem(tp, NC)
    first_core = core == 0
    place = jnp.stack([lax.rem(fsdp, NX), tp // NC, core]).astype(jnp.int32)
    rows_total = local_rows * lax.axis_size("fsdp")
    mine = grads.transpose(0, 2, 1, 3)

    kept = jnp.where(first_core, mine[0], mine[1])
    given = swap_cores(jnp.where(first_core, mine[1], mine[0]))
    chip = jnp.concatenate(
        [jnp.where(first_core, kept, given), jnp.where(first_core, given, kept)], axis=-1
    )

    to_send = jnp.broadcast_to(roots[None], (NX,) + roots.shape).reshape((NX * NC,) + roots.shape[1:])
    near = lax.all_to_all(to_send, AXES, 0, 0, axis_index_groups=GROUPS_XC)
    root_pieces = lax.all_gather(near, "fsdp", axis=0, axis_index_groups=GROUPS_Z)

    top = jnp.max(jnp.abs(mine)).astype(F32).reshape(1, 1)
    top = jnp.max(spread(jnp.max(spread(top, "tp"), axis=0), "fsdp"))
    scale = 32768.0 / (rows_total * jnp.maximum(top * top, 1e-34))

    pieces = []
    for j in range(blocks):
        own = chip[j]
        before, after = shift_y(own, 1), shift_y(own, -1)
        far_up = shift_y(halves(before)[0], 1)
        far_down = shift_y(halves(after)[1], -1)
        pieces.append((own, before, after, far_up, far_down))

    gradient = mine.astype(F32)
    adagrad = gradient / (jnp.sqrt(accum.transpose(0, 2, 1, 3) + gradient * gradient) + EPS)
    adagrad_sq = jnp.sum(adagrad * adagrad, axis=(2, 3))

    statistic = []
    for j in range(blocks):
        summed = reduce_x(gram_parts(place, pieces[j]), scale).astype(F16)
        rows = summed.shape[1]
        summed = summed.reshape(NZ, rows, NC, slab).transpose(0, 2, 1, 3).reshape(NZ * NC, rows, slab)
        terms = lax.all_to_all(summed, AXES, 0, 0, axis_index_groups=GROUPS_ZC)
        terms = terms.reshape(NZ, experts, rows, slab).astype(F32)
        statistic.append(jnp.sum(terms, axis=0) / (scale * rows_total))

    kept_part, given_part, direction_sq = [], [], []
    for j in range(blocks):
        value, other, squares = direction_of(place, pieces[j], root_pieces, j)
        kept_part.append(value)
        given_part.append(swap_cores(other))
        direction_sq.append(jnp.sum(squares[:, 0, 0]))
    direction_sq = jnp.stack(direction_sq)
    none = jnp.zeros_like(direction_sq)
    direction_sq = jnp.where(
        first_core, jnp.stack([direction_sq, none]), jnp.stack([none, direction_sq])
    )
    sums = jnp.stack([adagrad_sq, direction_sq])
    sums = jnp.sum(spread(jnp.sum(spread(sums, "tp"), axis=0), "fsdp"), axis=0)
    graft_scale = jnp.sqrt(sums[0]) / jnp.sqrt(sums[1] + 1e-06)
    kept_part, given_part = jnp.stack(kept_part), jnp.stack(given_part)
    step = jnp.stack(
        [
            jnp.where(first_core, kept_part, given_part) * graft_scale[0][:, None, None],
            jnp.where(first_core, given_part, kept_part) * graft_scale[1][:, None, None],
        ]
    )
    return (jnp.stack(statistic, axis=1), step.transpose(0, 2, 1, 3))


def solution(mesh):
    placed = (P(None, "fsdp", None, "tp"), P(None, "fsdp", None, "tp"), P(None, None, "fsdp", "tp"))
    return jax.shard_map(
        on_device,
        mesh=mesh,
        in_specs=placed,
        out_specs=(P(None, None, "fsdp", "tp"), P(None, "fsdp", None, "tp")),
        check_vma=False,
    )
```

```python
import functools
import jax
import jax.numpy as jnp
from jax import lax
from jax.experimental import pallas as pl
from jax.experimental.pallas import tpu as pltpu
from jax.sharding import PartitionSpec as P

EPS = 1e-08
NZ, NX, NY, NC = 8, 4, 4, 2
AXES = ("fsdp", "tp")
F32 = jnp.float32
F16 = jnp.float16
TAIL = 8
LARGEST = 14.0


def turn(c):
    return 1 - 2 * c


def device(z, x, y, c):
    return ((z * NX + x) * NY + y) * NC + c


EVERY = [(z, x, y, c) for z in range(NZ) for x in range(NX) for y in range(NY) for c in range(NC)]


def step_x(value, by):
    pairs = [(device(z, x, y, c), device(z, (x + by * turn(c)) % NX, y, c)) for z, x, y, c in EVERY]
    return lax.ppermute(value, AXES, pairs)


def step_y(value, by):
    pairs = [(y * NC + c, (y + by * turn(c)) % NY * NC + c) for y in range(NY) for c in range(NC)]
    return lax.ppermute(value, "tp", pairs)


def shift_x(value, by):
    pairs = [(z * NX + x, z * NX + (x + by) % NX) for z in range(NZ) for x in range(NX)]
    return lax.ppermute(value, "fsdp", pairs)


def swap_cores(value):
    return lax.ppermute(value, "tp", [(i, i ^ 1) for i in range(NY * NC)])


GROUPS_CZ = [
    [device(z, x, y, c) for c in range(NC) for z in range(NZ)] for x in range(NX) for y in range(NY)
]
GROUPS_Y = [[device(z, x, y, c) for y in range(NY) for c in range(NC)] for z in range(NZ) for x in range(NX)]
GROUPS_Z = [[device(z, x, y, c) for z in range(NZ)] for x in range(NX) for y in range(NY) for c in range(NC)]
RING_Z = [[z * NX + x for z in range(NZ)] for x in range(NX)]


def swap(value, dz, dx, dy, dc):
    pairs = [(device(z, x, y, c), device(z ^ dz, x ^ dx, y ^ dy, c ^ dc)) for z, x, y, c in EVERY]
    return lax.ppermute(value, AXES, pairs)


def spread(value, groups):
    copies = jnp.broadcast_to(value[None], (len(groups[0]),) + value.shape)
    return lax.all_to_all(copies, AXES, 0, 0, axis_index_groups=groups)


def after(value, *others):
    return lax.optimization_barrier((value,) + others)[0]


def contract_rows(a, b):
    return lax.dot_general(a, b, (((0,), (0,)), ((), ())), preferred_element_type=F32)


def gram_kernel(place, own, behind, beyond, ahead, cols, out):
    xi, yi, sense = place[0], place[1], 1 - 2 * place[2]
    rows = out.shape[3] - TAIL
    top = None
    for piece, dy in ((own, 0), (behind, -1), (beyond, -2), (ahead, 1)):
        part = lax.dot_general(
            piece[...], cols[...], (((0,), (0,)), ((), ())), preferred_element_type=F32
        )
        large = jnp.max(jnp.abs(part), axis=0, keepdims=True)
        top = large if top is None else jnp.maximum(top, large)
        y = lax.rem(yi + sense * dy + NY, NY)
        for i in range(2):
            for x in range(NX):
                first = (i * NX + x) * rows
                to = lax.rem((x - xi) * sense + NX, NX)
                out[to, 0, 2 * y + i, :rows] = part[first : first + rows]
    code = jnp.ceil(jnp.log2(jnp.clip(top, 2.0**-100, 2.0**100)))
    factor = jnp.exp2(LARGEST - code)
    tail = jnp.broadcast_to(code, (TAIL, code.shape[1]))
    for to in range(NX):
        for z in range(NZ):
            out[to, 0, z, :rows] = out[to, 0, z, :rows] * factor
            out[to, 0, z, rows:] = tail


def gram_parts(place, pieces):
    local_rows, wide = pieces[0].shape
    rows, cols = wide * NY // (NX * NZ), wide // NC
    whole = [pl.BlockSpec(piece.shape, lambda i, s: (0, 0)) for piece in pieces]
    return pl.pallas_call(
        gram_kernel,
        grid_spec=pltpu.PrefetchScalarGridSpec(
            num_scalar_prefetch=1,
            grid=(NC,),
            in_specs=whole + [pl.BlockSpec((local_rows, cols), lambda i, s: (0, i))],
            out_specs=pl.BlockSpec((NX, 1, NZ, rows + TAIL, cols), lambda i, s: (0, i, 0, 0, 0)),
        ),
        out_shape=jax.ShapeDtypeStruct((NX, NC, NZ, rows + TAIL, cols), F32),
        compiler_params=pltpu.CompilerParams(vmem_limit_bytes=32 << 20),
        cost_estimate=pl.CostEstimate(
            flops=2 * local_rows * wide * wide * NY,
            bytes_accessed=2 * local_rows * wide * NY + 4 * wide * wide * NY,
            transcendentals=0,
        ),
    )(place, *pieces, pieces[0])


def add_scaled(*terms):
    codes = [term[:, :1, -1:] for term in terms]
    code = functools.reduce(jnp.maximum, codes) + (len(terms) - 1)
    total = sum(term * jnp.exp2(own - code) for term, own in zip(terms, codes))
    in_tail = lax.broadcasted_iota(jnp.int32, total.shape, 2) >= total.shape[2] - TAIL
    return jnp.where(in_tail, code, total)


def direction_kernel(blocks, place, *refs):
    pieces, roots = refs[: NY * blocks], refs[NY * blocks]
    mine, theirs, squares, whole, root, sems = refs[NY * blocks + 1 :]
    xi, yi, ci = place[0], place[1], place[2]
    sense = 1 - 2 * ci
    wide, slab = root.shape[-1], mine.shape[-1]
    copies = []
    for j in range(blocks):
        group = [(roots.at[:, dx, j], root.at[j, :, lax.rem(xi + dx, NX)]) for dx in range(NX)]
        group += [(pieces[NY * j + k], whole.at[j, k]) for k in range(NY)]
        copies.append(
            [pltpu.make_async_copy(a, b, sems.at[j, i]) for i, (a, b) in enumerate(group)]
        )
    for group in copies:
        for copy in group:
            copy.start()
    for j in range(blocks):
        for copy in copies[j]:
            copy.wait()
        value = None
        for k, dy in enumerate((0, -1, -2, 1)):
            y = lax.rem(yi + sense * dy + NY, NY)
            b = root[j, pl.ds(2 * y, 2)].reshape(wide, wide)
            term = jnp.dot(whole[j, k], b, preferred_element_type=F32)
            value = term if value is None else value + term
        first, second = value[:, :slab], value[:, slab:]
        mine[j] = jnp.where(ci == 0, first, second)
        theirs[j] = jnp.where(ci == 0, second, first)
        squares[j] = jnp.full((8, 128), jnp.sum(value * value), F32)


def direction_of(place, pieces, roots):
    blocks = len(pieces)
    local_rows, wide = pieces[0][0].shape
    rows, slab = roots.shape[3], wide // NC
    result = jax.ShapeDtypeStruct((blocks, local_rows, slab), F32)
    vmem = pl.BlockSpec(memory_space=pltpu.VMEM)
    return pl.pallas_call(
        functools.partial(direction_kernel, blocks),
        in_specs=[pl.BlockSpec(memory_space=pltpu.SMEM)]
        + [pl.BlockSpec(memory_space=pltpu.HBM)] * (NY * blocks + 1),
        out_specs=[vmem, vmem, vmem],
        out_shape=[result, result, jax.ShapeDtypeStruct((blocks, 8, 128), F32)],
        scratch_shapes=[
            pltpu.VMEM((blocks, NY, local_rows, wide), jnp.bfloat16),
            pltpu.VMEM((blocks, NZ, NX, rows, wide), jnp.bfloat16),
            pltpu.SemaphoreType.DMA((blocks, NX + NY)),
        ],
        compiler_params=pltpu.CompilerParams(vmem_limit_bytes=60 << 20),
        cost_estimate=pl.CostEstimate(
            flops=2 * blocks * local_rows * wide * wide * NY,
            bytes_accessed=2 * blocks * (local_rows + wide) * wide * NY + 4 * blocks * local_rows * wide,
            transcendentals=0,
        ),
    )(place, *[piece for group in pieces for piece in group], roots)


def step_kernel(place, scale, kept, given, out):
    core, j = place[2], pl.program_id(0)
    out[core, 0] = kept[0] * scale[core, j]
    out[1 - core, 0] = given[0] * scale[1 - core, j]


def scaled_step(place, scale, kept, given):
    blocks, local_rows, slab = kept.shape
    return pl.pallas_call(
        step_kernel,
        grid=(blocks,),
        in_specs=[pl.BlockSpec(memory_space=pltpu.SMEM)] * 2
        + [pl.BlockSpec((1, local_rows, slab), lambda j: (j, 0, 0))] * 2,
        out_specs=pl.BlockSpec((NC, 1, local_rows, slab), lambda j: (0, j, 0, 0)),
        out_shape=jax.ShapeDtypeStruct((NC, blocks, local_rows, slab), F32),
        compiler_params=pltpu.CompilerParams(vmem_limit_bytes=32 << 20),
        cost_estimate=pl.CostEstimate(
            flops=2 * blocks * local_rows * slab,
            bytes_accessed=16 * blocks * local_rows * slab,
            transcendentals=0,
        ),
    )(place, scale, kept, given)


def on_device(grads, accum, roots):
    experts, local_rows, blocks, slab = grads.shape
    fsdp, tp = lax.axis_index("fsdp"), lax.axis_index("tp")
    core = lax.rem(tp, NC)
    first_core = core == 0
    place = jnp.stack([lax.rem(fsdp, NX), tp // NC, core]).astype(jnp.int32)
    rows_total = local_rows * lax.axis_size("fsdp")
    mine = grads.transpose(0, 2, 1, 3)

    def pick(pair):
        return jnp.where(first_core, pair[0], pair[1]), jnp.where(first_core, pair[1], pair[0])

    def by_core(kept, given):
        return jnp.concatenate(pick((kept, given)), axis=-1)

    (kept_grads, other_grads), (kept_roots, other_roots) = pick(mine), pick(roots)
    given = swap_cores(jnp.concatenate([other_grads, other_roots], axis=1))
    given_grads, given_roots = given[:, :local_rows], given[:, local_rows:]

    chip = [by_core(kept_grads[j], given_grads[j]) for j in range(blocks)]
    root = by_core(kept_roots, given_roots)
    chip[0], chip[1], chip[2], root = lax.optimization_barrier((*chip, root))

    def send_near(own):
        return step_y(own, 1), step_y(own, -1)

    near = [send_near(chip[0])]
    root = [root, shift_x(root, -1), shift_x(root, 2), shift_x(root, 1)]
    root = jnp.stack(lax.optimization_barrier((*root, *near[0]))[:NX])
    root_pieces = lax.all_gather(root, "fsdp", axis=0, axis_index_groups=RING_Z)

    near.append(send_near(after(chip[1], *near[0])))
    near.append(send_near(after(chip[2], *near[1])))
    gradient = mine.astype(F32)
    adagrad = gradient / (jnp.sqrt(accum.transpose(0, 2, 1, 3) + gradient * gradient) + EPS)
    adagrad_sq = jnp.sum(adagrad * adagrad, axis=(2, 3))

    def collect(j, *wait):
        behind = after(near[j][0], *wait) if wait else near[j][0]
        return chip[j], near[j][0], step_y(behind, 1), near[j][1]

    def send_first(part):
        return step_x(part[2].astype(F16), 1), step_x(part[3].astype(F16), -1)

    def onward(part, arrived):
        return add_scaled(part[1], arrived[0].astype(F32)).astype(F16)

    def send_second(value, arrived):
        return step_x(value, 1), arrived[1]

    def owned(part, arrived):
        return add_scaled(part[0], arrived[0].astype(F32), arrived[1].astype(F32)).astype(F16)

    def send_rows(summed):
        summed = summed.reshape(NC * NZ, -1, slab)
        return lax.all_to_all(summed, AXES, 0, 0, axis_index_groups=GROUPS_CZ)

    def add_rows(term):
        term = term.reshape(experts, NZ, -1, slab).astype(F32)
        factor = jnp.exp2(term[:, :, -1:] - LARGEST)
        return jnp.sum(term[:, :, :-TAIL] * factor, axis=1) / rows_total

    pieces = [collect(0), collect(1)]
    part0 = gram_parts(after(place, *near[1]), pieces[0])
    pieces.append(collect(2))
    got0 = send_first(part0)
    part1 = gram_parts(after(place, part0, *near[2]), pieces[1])
    got1 = send_first(part1)
    value0 = onward(part0, after(got0, part1))
    got0 = send_second(value0, got0)
    part2 = gram_parts(after(place, value0), pieces[2])
    got2 = send_first(part2)
    value1 = onward(part1, after(got1, part2))
    got1 = send_second(value1, got1)
    rows0 = owned(part0, after(got0, value1))
    terms = [send_rows(rows0)]
    kept_part, given_part, squares = direction_of(after(place, rows0), pieces, root_pieces)
    given_part = swap_cores(given_part)
    value2 = onward(part2, after(got2, squares))
    got2 = send_second(value2, got2)

    direction_sq = squares[:, 0, 0]
    none = jnp.zeros_like(direction_sq)
    direction_sq = jnp.where(
        first_core, jnp.stack([direction_sq, none]), jnp.stack([none, direction_sq])
    )
    sums = after(jnp.stack([adagrad_sq, direction_sq]), terms[0])
    sums = jnp.sum(spread(sums, GROUPS_Y), axis=0)
    rows1 = owned(part1, after(got1, value2, sums))
    terms.append(send_rows(rows1))
    sums = sums + swap(sums, 0, 1, 0, 0)
    sums = sums + swap(sums, 0, 2, 0, 0)
    rows2 = owned(part2, after(got2, rows1, sums))
    sums = jnp.sum(spread(after(sums, terms[1]), GROUPS_Z), axis=0)
    terms.append(send_rows(after(rows2, sums)))
    statistic = jnp.stack([add_rows(term) for term in terms], axis=1)
    graft_scale = jnp.sqrt(sums[0]) / jnp.sqrt(sums[1] + 1e-06)
    step = scaled_step(place, graft_scale, kept_part, given_part)
    return (statistic, step.transpose(0, 2, 1, 3))


def solution(mesh):
    placed = (P(None, "fsdp", None, "tp"), P(None, "fsdp", None, "tp"), P(None, None, "fsdp", "tp"))
    return jax.shard_map(
        on_device,
        mesh=mesh,
        in_specs=placed,
        out_specs=(P(None, None, "fsdp", "tp"), P(None, "fsdp", None, "tp")),
        check_vma=False,
    )
```

```python
import functools
import jax
import jax.numpy as jnp
from jax import lax
from jax.experimental import pallas as pl
from jax.experimental.pallas import tpu as pltpu
from jax.sharding import PartitionSpec as P

EPS = 1e-08
NZ, NX, NY, NC = 8, 4, 4, 2
AXES = ("fsdp", "tp")
F32 = jnp.float32
F16 = jnp.float16
TAIL = 8
LARGEST = 14.0
LOW = 256.0


def turn(c):
    return 1 - 2 * c


def device(z, x, y, c):
    return ((z * NX + x) * NY + y) * NC + c


EVERY = [(z, x, y, c) for z in range(NZ) for x in range(NX) for y in range(NY) for c in range(NC)]


def step_x(value, by):
    pairs = [(device(z, x, y, c), device(z, (x + by * turn(c)) % NX, y, c)) for z, x, y, c in EVERY]
    return lax.ppermute(value, AXES, pairs)


def step_y(value, by):
    pairs = [(y * NC + c, (y + by * turn(c)) % NY * NC + c) for y in range(NY) for c in range(NC)]
    return lax.ppermute(value, "tp", pairs)


def shift_x(value, by):
    pairs = [(z * NX + x, z * NX + (x + by) % NX) for z in range(NZ) for x in range(NX)]
    return lax.ppermute(value, "fsdp", pairs)


def swap_cores(value):
    return lax.ppermute(value, "tp", [(i, i ^ 1) for i in range(NY * NC)])


GROUPS_CZ = [
    [device(z, x, y, c) for c in range(NC) for z in range(NZ)] for x in range(NX) for y in range(NY)
]
GROUPS_Y = [[device(z, x, y, c) for y in range(NY) for c in range(NC)] for z in range(NZ) for x in range(NX)]
GROUPS_Z = [[device(z, x, y, c) for z in range(NZ)] for x in range(NX) for y in range(NY) for c in range(NC)]
RING_Z = [[z * NX + x for z in range(NZ)] for x in range(NX)]


def swap_cores(value):
    return lax.ppermute(value, "tp", [(i, i ^ 1) for i in range(NY * NC)])


GROUPS_CZ = [
    [device(z, x, y, c) for c in range(NC) for z in range(NZ)] for x in range(NX) for y in range(NY)
]
GROUPS_Y = [[device(z, x, y, c) for y in range(NY) for c in range(NC)] for z in range(NZ) for x in range(NX)]
GROUPS_Z = [[device(z, x, y, c) for z in range(NZ)] for x in range(NX) for y in range(NY) for c in range(NC)]
RING_Z = [[z * NX + x for z in range(NZ)] for x in range(NX)]


SWAPS = (
    (0, 2, 0, 0),
    (0, 1, 0, 0),
    (0, 0, 2, 0),
    (0, 0, 1, 0),
)


def swap(value, dz, dx, dy, dc):
    pairs = [(device(z, x, y, c), device(z ^ dz, x ^ dx, y ^ dy, c ^ dc)) for z, x, y, c in EVERY]
    return lax.ppermute(value, AXES, pairs)


def spread(value, groups):
    copies = jnp.broadcast_to(value[None], (len(groups[0]),) + value.shape)
    return lax.all_to_all(copies, AXES, 0, 0, axis_index_groups=groups)


def after(value, *others):
    return lax.optimization_barrier((value,) + others)[0]


def contract_rows(a, b):
    return lax.dot_general(a, b, (((0,), (0,)), ((), ())), preferred_element_type=F32)


def gram_kernel(place, own, behind, beyond, ahead, cols, *refs):
    outs, terms = refs[:NX], refs[NX]
    xi, yi, sense = place[0], place[1], 1 - 2 * place[2]
    rows = terms.shape[2]
    top = None
    for piece, dy in ((own, 0), (behind, -1), (beyond, -2), (ahead, 1)):
        part = lax.dot_general(
            piece[...], cols[...], (((0,), (0,)), ((), ())), preferred_element_type=F32
        )
        large = jnp.max(jnp.abs(part), axis=0, keepdims=True)
        top = large if top is None else jnp.maximum(top, large)
        y = lax.rem(yi + sense * dy + NY, NY)
        for i in range(2):
            for x in range(NX):
                first = (i * NX + x) * rows
                to = lax.rem((x - xi) * sense + NX, NX)
                terms[to, 2 * y + i] = part[first : first + rows]
    code = jnp.ceil(jnp.log2(jnp.clip(top, 2.0**-100, 2.0**100)))
    factor = jnp.exp2(LARGEST - code)
    tail = jnp.broadcast_to(code, (TAIL, code.shape[1]))
    for to, out in enumerate(outs):
        for z in range(NZ):
            out[0, z, :rows] = terms[to, z] * factor
            out[0, z, rows:] = tail


def gram_parts(place, pieces):
    local_rows, wide = pieces[0].shape
    rows, cols = wide * NY // (NX * NZ), wide // NC
    whole = [pl.BlockSpec(piece.shape, lambda i, s: (0, 0)) for piece in pieces]
    shape = (NC, NZ, rows + TAIL, cols)
    return pl.pallas_call(
        gram_kernel,
        grid_spec=pltpu.PrefetchScalarGridSpec(
            num_scalar_prefetch=1,
            grid=(NC,),
            in_specs=whole + [pl.BlockSpec((local_rows, cols), lambda i, s: (0, i))],
            out_specs=[pl.BlockSpec((1,) + shape[1:], lambda i, s: (i, 0, 0, 0))] * NX,
            scratch_shapes=[pltpu.VMEM((NX, NZ, rows, cols), F32)],
        ),
        out_shape=[jax.ShapeDtypeStruct(shape, F32)] * NX,
        compiler_params=pltpu.CompilerParams(vmem_limit_bytes=32 << 20),
        cost_estimate=pl.CostEstimate(
            flops=2 * local_rows * wide * wide * NY,
            bytes_accessed=2 * local_rows * wide * NY + 4 * wide * wide * NY,
            transcendentals=0,
        ),
    )(place, *pieces, pieces[0])


def power(code):
    return jnp.left_shift(1, 30 + jnp.maximum(code, -30.0).astype(jnp.int32)).astype(F32) * 2.0**-30


def add_scaled(*terms, note=None):
    codes = [term[:, :1, -1:].astype(F32) for term in terms]
    code = functools.reduce(jnp.maximum, codes) + (len(terms) - 1)
    total = sum(term.astype(F32) * power(own - code) for term, own in zip(terms, codes))
    row = lax.broadcasted_iota(jnp.int32, total.shape, 2)
    rest = code if note is None else jnp.where(row == total.shape[2] - 1, code, note)
    return jnp.where(row >= total.shape[2] - TAIL, rest, total).astype(F16)


def direction_kernel(blocks, place, adagrad, *refs):
    pieces, roots = refs[: NY * blocks], refs[NY * blocks]
    mine, theirs, note, whole, root, sems = refs[NY * blocks + 1 :]
    xi, yi, ci = place[0], place[1], place[2]
    sense = 1 - 2 * ci
    wide, slab = root.shape[-1], mine.shape[-1]
    copies = []
    for j in range(blocks):
        group = [(roots.at[:, dx, j], root.at[j, :, lax.rem(xi + dx, NX)]) for dx in range(NX)]
        for k, dy in enumerate((0, -1, -2, 1)):
            start = pl.multiple_of(lax.rem(yi + sense * dy + NY, NY) * wide, wide)
            group.append((pieces[NY * j + k], whole.at[j, :, pl.ds(start, wide)]))
        copies.append(
            [pltpu.make_async_copy(a, b, sems.at[j, i]) for i, (a, b) in enumerate(group)]
        )
    for copy in copies[0]:
        copy.start()
    sums = [adagrad[e, j] for e in range(NC) for j in range(blocks)]
    for j in range(blocks):
        if j + 1 < blocks:
            for copy in copies[j + 1]:
                copy.start()
        for copy in copies[j]:
            copy.wait()
        value = jnp.dot(
            whole[j], root[j].reshape(NY * wide, wide), preferred_element_type=F32
        )
        first, second = value[:, :slab], value[:, slab:]
        mine[j] = jnp.where(ci == 0, first, second)
        theirs[j] = jnp.where(ci == 0, second, first)
        sums.append(jnp.sum(value * value))
    lane = lax.broadcasted_iota(jnp.int32, (1, note.shape[1]), 1)
    line = jnp.zeros(lane.shape, F32)
    for i, value in enumerate(sums):
        line = jnp.where(lane == i, value, line)
    code = jnp.ceil(jnp.log2(jnp.clip(line, 2.0**-100, 2.0**100)))
    line = line * jnp.exp2(-code)
    high = line.astype(jnp.bfloat16).astype(F32)
    rows = note.shape[0] - TAIL
    note[...] = jnp.zeros(note.shape, F32)
    for i, value in enumerate((code, high, (line - high) * LOW)):
        note[rows + i : rows + i + 1] = value


def direction_of(place, adagrad_sq, pieces, roots):
    blocks = len(pieces)
    local_rows, wide = pieces[0][0].shape
    rows, slab = roots.shape[3], wide // NC
    result = jax.ShapeDtypeStruct((blocks, local_rows, slab), F32)
    vmem = pl.BlockSpec(memory_space=pltpu.VMEM)
    return pl.pallas_call(
        functools.partial(direction_kernel, blocks),
        in_specs=[pl.BlockSpec(memory_space=pltpu.SMEM)] * 2
        + [pl.BlockSpec(memory_space=pltpu.HBM)] * (NY * blocks + 1),
        out_specs=[vmem, vmem, vmem],
        out_shape=[result, result, jax.ShapeDtypeStruct((rows + TAIL, slab), F32)],
        scratch_shapes=[
            pltpu.VMEM((blocks, local_rows, NY * wide), jnp.bfloat16),
            pltpu.VMEM((blocks, NZ, NX, rows, wide), jnp.bfloat16),
            pltpu.SemaphoreType.DMA((blocks, NX + NY)),
        ],
        compiler_params=pltpu.CompilerParams(vmem_limit_bytes=60 << 20),
        cost_estimate=pl.CostEstimate(
            flops=2 * blocks * local_rows * wide * wide * NY,
            bytes_accessed=2 * blocks * (local_rows + wide) * wide * NY + 4 * blocks * local_rows * wide,
            transcendentals=0,
        ),
    )(place, adagrad_sq, *[piece for group in pieces for piece in group], roots)


def step_kernel(place, scale, kept, given, out):
    core, j = place[2], pl.program_id(0)
    out[core, 0] = kept[0] * scale[core, j]
    out[1 - core, 0] = given[0] * scale[1 - core, j]


def scaled_step(place, scale, kept, given):
    blocks, local_rows, slab = kept.shape
    return pl.pallas_call(
        step_kernel,
        grid=(blocks,),
        in_specs=[pl.BlockSpec(memory_space=pltpu.SMEM)] * 2
        + [pl.BlockSpec((1, local_rows, slab), lambda j: (j, 0, 0))] * 2,
        out_specs=pl.BlockSpec((NC, 1, local_rows, slab), lambda j: (0, j, 0, 0)),
        out_shape=jax.ShapeDtypeStruct((NC, blocks, local_rows, slab), F32),
        compiler_params=pltpu.CompilerParams(vmem_limit_bytes=32 << 20),
        cost_estimate=pl.CostEstimate(
            flops=2 * blocks * local_rows * slab,
            bytes_accessed=16 * blocks * local_rows * slab,
            transcendentals=0,
        ),
    )(place, scale, kept, given)


def on_device(grads, accum, roots):
    experts, local_rows, blocks, slab = grads.shape
    fsdp, tp = lax.axis_index("fsdp"), lax.axis_index("tp")
    core = lax.rem(tp, NC)
    first_core = core == 0
    place = jnp.stack([lax.rem(fsdp, NX), tp // NC, core]).astype(jnp.int32)
    rows_total = local_rows * lax.axis_size("fsdp")
    mine = grads.transpose(0, 2, 1, 3)

    def pick(pair):
        return jnp.where(first_core, pair[0], pair[1]), jnp.where(first_core, pair[1], pair[0])

    def by_core(kept, given):
        return jnp.concatenate(pick((kept, given)), axis=-1)

    (kept_grads, other_grads), (kept_roots, other_roots) = pick(mine), pick(roots)
    given = swap_cores(jnp.concatenate([other_grads, other_roots], axis=1))
    given_grads, given_roots = given[:, :local_rows], given[:, local_rows:]

    chip = [by_core(kept_grads[j], given_grads[j]) for j in range(blocks)]
    root = by_core(kept_roots, given_roots)
    chip[0], chip[1], chip[2], root = lax.optimization_barrier((*chip, root))

    def send_near(own):
        return step_y(own, 1), step_y(own, -1)

    near = [send_near(chip[0])]
    root = [root, shift_x(root, -1), shift_x(root, 2), shift_x(root, 1)]
    root = jnp.stack(lax.optimization_barrier((*root, *near[0]))[:NX])
    root_pieces = lax.all_gather(root, "fsdp", axis=0, axis_index_groups=RING_Z)

    near.append(send_near(after(chip[1], *near[0])))
    gradient = mine.astype(F32)
    adagrad = gradient / (jnp.sqrt(accum.transpose(0, 2, 1, 3) + gradient * gradient) + EPS)
    adagrad_sq = jnp.sum(adagrad * adagrad, axis=(2, 3))

    def collect(j, *wait):
        behind = after(near[j][0], *wait) if wait else near[j][0]
        return chip[j], near[j][0], step_y(behind, 1), near[j][1]

    def send_first(part):
        return step_x(part[2].astype(F16), 1), step_x(part[3].astype(F16), -1)

    def onward(part, arrived):
        return add_scaled(part[1], arrived[0])

    def send_second(value, arrived):
        return step_x(value, 1), arrived[1]

    def owned(part, arrived, note=None):
        return add_scaled(part[0], *arrived, note=note)

    def send_rows(summed):
        summed = summed.reshape((NC * NZ,) + summed.shape[2:])
        return lax.all_to_all(summed, AXES, 0, 0, axis_index_groups=GROUPS_CZ)

    def add_rows(term):
        term = term.reshape((experts, NZ) + term.shape[1:])
        factor = jnp.exp2(term[..., -1:, :].astype(F32) - LARGEST)
        return jnp.sum(term[..., :-TAIL, :].astype(F32) * factor, axis=1) / rows_total

    pieces = [collect(0), collect(1)]
    near.append(send_near(after(chip[2], pieces[1][2])))
    pieces.append(collect(2))
    part0 = gram_parts(after(place, adagrad_sq, *near[1]), pieces[0])
    got0 = send_first(part0)
    part1 = gram_parts(after(place, part0[0]), pieces[1])
    got1 = send_first(part1)
    value0 = onward(part0, after(got0, part1[0], *near[2]))
    got0 = send_second(value0, got0)
    part2 = gram_parts(after(place, value0), pieces[2])
    got2 = send_first(part2)
    value1 = onward(part1, after(got1, part2[0]))
    got1 = send_second(value1, got1)
    rows0 = owned(part0, after(got0, value1))
    terms = [send_rows(rows0)]
    kept_part, given_part, note = direction_of(after(place, rows0, *got2), adagrad_sq, pieces, root_pieces)
    given_part = swap_cores(given_part)
    value2 = onward(part2, after(got2, note))
    got2 = send_second(value2, got2)
    rows1 = owned(part1, after(got1, value2), note)
    terms.append(send_rows(rows1))
    terms[0] = after(terms[0], rows1)
    sums = terms[1][:, -TAIL : 3 - TAIL].astype(F32)
    sums = (sums[:, 1] + sums[:, 2] / LOW) * jnp.exp2(sums[:, 0])
    sums = jnp.sum(sums.reshape(experts, NZ, slab), axis=1)
    rows2 = owned(part2, after(got2, terms[1]))
    terms.append(send_rows(rows2))
    sums = sums + step_x(sums, 1) + step_x(sums, -1) + step_x(sums, 2)
    sums = sums + step_y(sums, 1) + step_y(sums, -1) + step_y(sums, 2)
    count = experts * blocks
    sums = jnp.sum(sums[:, :count], axis=0).reshape(experts, blocks), sums[:, count : count + blocks]
    statistic = jnp.stack([add_rows(term) for term in terms], axis=1)
    graft_scale = jnp.sqrt(sums[0]) / jnp.sqrt(sums[1] + 1e-06)
    step = scaled_step(place, graft_scale, kept_part, given_part)
    return (statistic, step.transpose(0, 2, 1, 3))


def solution(mesh):
    placed = (P(None, "fsdp", None, "tp"), P(None, "fsdp", None, "tp"), P(None, None, "fsdp", "tp"))
    return jax.shard_map(
        on_device,
        mesh=mesh,
        in_specs=placed,
        out_specs=(P(None, None, "fsdp", "tp"), P(None, "fsdp", None, "tp")),
        check_vma=False,
    )
```

```python
import functools
import jax
import jax.numpy as jnp
from jax import lax
from jax.experimental import pallas as pl
from jax.experimental.pallas import tpu as pltpu
from jax.sharding import PartitionSpec as P

EPS = 1e-08
NZ, NX, NY, NC = 8, 4, 4, 2
AXES = ("fsdp", "tp")
F32 = jnp.float32
F16 = jnp.float16
TAIL = 8
LARGEST = 14.0
LOW = 256.0


def turn(c):
    return 1 - 2 * c


def device(z, x, y, c):
    return ((z * NX + x) * NY + y) * NC + c


EVERY = [(z, x, y, c) for z in range(NZ) for x in range(NX) for y in range(NY) for c in range(NC)]


def step_x(value, by):
    pairs = [(device(z, x, y, c), device(z, (x + by * turn(c)) % NX, y, c)) for z, x, y, c in EVERY]
    return lax.ppermute(value, AXES, pairs)


def step_y(value, by):
    pairs = [(y * NC + c, (y + by * turn(c)) % NY * NC + c) for y in range(NY) for c in range(NC)]
    return lax.ppermute(value, "tp", pairs)


def shift_x(value, by):
    pairs = [(z * NX + x, z * NX + (x + by) % NX) for z in range(NZ) for x in range(NX)]
    return lax.ppermute(value, "fsdp", pairs)


def swap_cores(value):
    return lax.ppermute(value, "tp", [(i, i ^ 1) for i in range(NY * NC)])


GROUPS_CZ = [
    [device(z, x, y, c) for c in range(NC) for z in range(NZ)] for x in range(NX) for y in range(NY)
]
GROUPS_Y = [[device(z, x, y, c) for y in range(NY) for c in range(NC)] for z in range(NZ) for x in range(NX)]
GROUPS_Z = [[device(z, x, y, c) for z in range(NZ)] for x in range(NX) for y in range(NY) for c in range(NC)]
RING_Z = [[z * NX + x for z in range(NZ)] for x in range(NX)]


def swap_cores(value):
    return lax.ppermute(value, "tp", [(i, i ^ 1) for i in range(NY * NC)])


GROUPS_CZ = [
    [device(z, x, y, c) for c in range(NC) for z in range(NZ)] for x in range(NX) for y in range(NY)
]
GROUPS_Y = [[device(z, x, y, c) for y in range(NY) for c in range(NC)] for z in range(NZ) for x in range(NX)]
GROUPS_Z = [[device(z, x, y, c) for z in range(NZ)] for x in range(NX) for y in range(NY) for c in range(NC)]
RING_Z = [[z * NX + x for z in range(NZ)] for x in range(NX)]


SWAPS = (
    (0, 2, 0, 0),
    (0, 1, 0, 0),
    (0, 0, 2, 0),
    (0, 0, 1, 0),
)


def swap(value, dz, dx, dy, dc):
    pairs = [(device(z, x, y, c), device(z ^ dz, x ^ dx, y ^ dy, c ^ dc)) for z, x, y, c in EVERY]
    return lax.ppermute(value, AXES, pairs)


def spread(value, groups):
    copies = jnp.broadcast_to(value[None], (len(groups[0]),) + value.shape)
    return lax.all_to_all(copies, AXES, 0, 0, axis_index_groups=groups)


def after(value, *others):
    return lax.optimization_barrier((value,) + others)[0]


def contract_rows(a, b):
    return lax.dot_general(a, b, (((0,), (0,)), ((), ())), preferred_element_type=F32)


def gram_kernel(place, own, behind, beyond, ahead, cols, *refs):
    outs, terms = refs[:NX], refs[NX]
    xi, yi, sense = place[0], place[1], 1 - 2 * place[2]
    rows = terms.shape[2]
    top = None
    for piece, dy in ((own, 0), (behind, -1), (beyond, -2), (ahead, 1)):
        part = lax.dot_general(
            piece[...], cols[...], (((0,), (0,)), ((), ())), preferred_element_type=F32
        )
        large = jnp.max(jnp.abs(part), axis=0, keepdims=True)
        top = large if top is None else jnp.maximum(top, large)
        y = lax.rem(yi + sense * dy + NY, NY)
        for i in range(2):
            for x in range(NX):
                first = (i * NX + x) * rows
                to = lax.rem((x - xi) * sense + NX, NX)
                terms[to, 2 * y + i] = part[first : first + rows]
    code = jnp.ceil(jnp.log2(jnp.clip(top, 2.0**-100, 2.0**100)))
    factor = jnp.exp2(LARGEST - code)
    tail = jnp.broadcast_to(code, (TAIL, code.shape[1]))
    for to, out in enumerate(outs):
        for z in range(NZ):
            out[0, z, :rows] = terms[to, z] * factor
            out[0, z, rows:] = tail


def gram_parts(place, pieces):
    local_rows, wide = pieces[0].shape
    rows, cols = wide * NY // (NX * NZ), wide // NC
    whole = [pl.BlockSpec(piece.shape, lambda i, s: (0, 0)) for piece in pieces]
    shape = (NC, NZ, rows + TAIL, cols)
    return pl.pallas_call(
        gram_kernel,
        grid_spec=pltpu.PrefetchScalarGridSpec(
            num_scalar_prefetch=1,
            grid=(NC,),
            in_specs=whole + [pl.BlockSpec((local_rows, cols), lambda i, s: (0, i))],
            out_specs=[pl.BlockSpec((1,) + shape[1:], lambda i, s: (i, 0, 0, 0))] * NX,
            scratch_shapes=[pltpu.VMEM((NX, NZ, rows, cols), F32)],
        ),
        out_shape=[jax.ShapeDtypeStruct(shape, F32)] * NX,
        compiler_params=pltpu.CompilerParams(vmem_limit_bytes=32 << 20),
        cost_estimate=pl.CostEstimate(
            flops=2 * local_rows * wide * wide * NY,
            bytes_accessed=2 * local_rows * wide * NY + 4 * wide * wide * NY,
            transcendentals=0,
        ),
    )(place, *pieces, pieces[0])


def power(code):
    return jnp.left_shift(1, 30 + jnp.maximum(code, -30.0).astype(jnp.int32)).astype(F32) * 2.0**-30


def add_scaled(*terms, note=None):
    codes = [term[:, :1, -1:].astype(F32) for term in terms]
    code = functools.reduce(jnp.maximum, codes) + (len(terms) - 1)
    total = sum(term.astype(F32) * power(own - code) for term, own in zip(terms, codes))
    row = lax.broadcasted_iota(jnp.int32, total.shape, 2)
    rest = code if note is None else jnp.where(row == total.shape[2] - 1, code, note)
    return jnp.where(row >= total.shape[2] - TAIL, rest, total).astype(F16)


def direction_kernel(blocks, place, adagrad, *refs):
    pieces, roots = refs[: NY * blocks], refs[NY * blocks]
    mine, theirs, note, whole, root, sems = refs[NY * blocks + 1 :]
    xi, yi, ci = place[0], place[1], place[2]
    sense = 1 - 2 * ci
    wide, slab = root.shape[-1], mine.shape[-1]
    copies = []
    for j in range(blocks):
        group = [(roots.at[:, dx, j], root.at[j, :, lax.rem(xi + dx, NX)]) for dx in range(NX)]
        for k, dy in enumerate((0, -1, -2, 1)):
            start = pl.multiple_of(lax.rem(yi + sense * dy + NY, NY) * wide, wide)
            group.append((pieces[NY * j + k], whole.at[j, :, pl.ds(start, wide)]))
        copies.append(
            [pltpu.make_async_copy(a, b, sems.at[j, i]) for i, (a, b) in enumerate(group)]
        )
    for copy in copies[0]:
        copy.start()
    sums = [adagrad[e, j] for e in range(NC) for j in range(blocks)]
    for j in range(blocks):
        if j + 1 < blocks:
            for copy in copies[j + 1]:
                copy.start()
        for copy in copies[j]:
            copy.wait()
        value = jnp.dot(
            whole[j], root[j].reshape(NY * wide, wide), preferred_element_type=F32
        )
        first, second = value[:, :slab], value[:, slab:]
        mine[j] = jnp.where(ci == 0, first, second)
        theirs[j] = jnp.where(ci == 0, second, first)
        sums.append(jnp.sum(value * value))
    lane = lax.broadcasted_iota(jnp.int32, (1, note.shape[1]), 1)
    line = jnp.zeros(lane.shape, F32)
    for i, value in enumerate(sums):
        line = jnp.where(lane == i, value, line)
    code = jnp.ceil(jnp.log2(jnp.clip(line, 2.0**-100, 2.0**100)))
    line = line * jnp.exp2(-code)
    high = line.astype(jnp.bfloat16).astype(F32)
    rows = note.shape[0] - TAIL
    note[...] = jnp.zeros(note.shape, F32)
    for i, value in enumerate((code, high, (line - high) * LOW)):
        note[rows + i : rows + i + 1] = value


def direction_of(place, adagrad_sq, pieces, roots):
    blocks = len(pieces)
    local_rows, wide = pieces[0][0].shape
    rows, slab = roots.shape[3], wide // NC
    result = jax.ShapeDtypeStruct((blocks, local_rows, slab), F32)
    vmem = pl.BlockSpec(memory_space=pltpu.VMEM)
    return pl.pallas_call(
        functools.partial(direction_kernel, blocks),
        in_specs=[pl.BlockSpec(memory_space=pltpu.SMEM)] * 2
        + [pl.BlockSpec(memory_space=pltpu.HBM)] * (NY * blocks + 1),
        out_specs=[vmem, vmem, vmem],
        out_shape=[result, result, jax.ShapeDtypeStruct((rows + TAIL, slab), F32)],
        scratch_shapes=[
            pltpu.VMEM((blocks, local_rows, NY * wide), jnp.bfloat16),
            pltpu.VMEM((blocks, NZ, NX, rows, wide), jnp.bfloat16),
            pltpu.SemaphoreType.DMA((blocks, NX + NY)),
        ],
        compiler_params=pltpu.CompilerParams(vmem_limit_bytes=60 << 20),
        cost_estimate=pl.CostEstimate(
            flops=2 * blocks * local_rows * wide * wide * NY,
            bytes_accessed=2 * blocks * (local_rows + wide) * wide * NY + 4 * blocks * local_rows * wide,
            transcendentals=0,
        ),
    )(place, adagrad_sq, *[piece for group in pieces for piece in group], roots)


def step_kernel(place, scale, kept, given, out):
    core, j = place[2], pl.program_id(0)
    out[core, 0] = kept[0] * scale[core, j]
    out[1 - core, 0] = given[0] * scale[1 - core, j]


def scaled_step(place, scale, kept, given):
    blocks, local_rows, slab = kept.shape
    return pl.pallas_call(
        step_kernel,
        grid=(blocks,),
        in_specs=[pl.BlockSpec(memory_space=pltpu.SMEM)] * 2
        + [pl.BlockSpec((1, local_rows, slab), lambda j: (j, 0, 0))] * 2,
        out_specs=pl.BlockSpec((NC, 1, local_rows, slab), lambda j: (0, j, 0, 0)),
        out_shape=jax.ShapeDtypeStruct((NC, blocks, local_rows, slab), F32),
        compiler_params=pltpu.CompilerParams(vmem_limit_bytes=32 << 20),
        cost_estimate=pl.CostEstimate(
            flops=2 * blocks * local_rows * slab,
            bytes_accessed=16 * blocks * local_rows * slab,
            transcendentals=0,
        ),
    )(place, scale, kept, given)


def on_device(grads, accum, roots):
    experts, local_rows, blocks, slab = grads.shape
    fsdp, tp = lax.axis_index("fsdp"), lax.axis_index("tp")
    core = lax.rem(tp, NC)
    first_core = core == 0
    place = jnp.stack([lax.rem(fsdp, NX), tp // NC, core]).astype(jnp.int32)
    rows_total = local_rows * lax.axis_size("fsdp")
    mine = grads.transpose(0, 2, 1, 3)

    def pick(pair):
        return jnp.where(first_core, pair[0], pair[1]), jnp.where(first_core, pair[1], pair[0])

    def by_core(kept, given):
        return jnp.concatenate(pick((kept, given)), axis=-1)

    (kept_grads, other_grads), (kept_roots, other_roots) = pick(mine), pick(roots)
    given = swap_cores(jnp.concatenate([other_grads, other_roots], axis=1))
    given_grads, given_roots = given[:, :local_rows], given[:, local_rows:]

    chip = [by_core(kept_grads[j], given_grads[j]) for j in range(blocks)]
    root = by_core(kept_roots, given_roots)
    chip[0], chip[1], chip[2], root = lax.optimization_barrier((*chip, root))

    def send_near(own):
        return step_y(own, 1), step_y(own, -1)

    near = [send_near(chip[0])]
    root = [root, shift_x(root, -1), shift_x(root, 2), shift_x(root, 1)]
    root = jnp.stack(lax.optimization_barrier((*root, *near[0]))[:NX])
    root_pieces = lax.all_gather(root, "fsdp", axis=0, axis_index_groups=RING_Z)

    near.append(send_near(after(chip[1], *near[0])))
    gradient = mine.astype(F32)
    adagrad = gradient / (jnp.sqrt(accum.transpose(0, 2, 1, 3) + gradient * gradient) + EPS)
    adagrad_sq = jnp.sum(adagrad * adagrad, axis=(2, 3))

    def collect(j, *wait):
        behind = after(near[j][0], *wait) if wait else near[j][0]
        return chip[j], near[j][0], step_y(behind, 1), near[j][1]

    def send_first(part):
        return step_x(part[2].astype(F16), 1), step_x(part[3].astype(F16), -1)

    def onward(part, arrived):
        return add_scaled(part[1], arrived[0])

    def send_second(value, arrived):
        return step_x(value, 1), arrived[1]

    def owned(part, arrived, note=None):
        return add_scaled(part[0], *arrived, note=note)

    def send_rows(summed):
        summed = summed.reshape((NC * NZ,) + summed.shape[2:])
        return lax.all_to_all(summed, AXES, 0, 0, axis_index_groups=GROUPS_CZ)

    def add_rows(term):
        term = term.reshape((experts, NZ) + term.shape[1:])
        factor = jnp.exp2(term[..., -1:, :].astype(F32) - LARGEST)
        return (jnp.sum(term.astype(F32) * factor, axis=1) / rows_total)[..., :-TAIL, :]

    pieces = [collect(0), collect(1)]
    near.append(send_near(after(chip[2], pieces[1][2])))
    pieces.append(collect(2))
    part0 = gram_parts(after(place, adagrad_sq, *near[1]), pieces[0])
    got0 = send_first(part0)
    part1 = gram_parts(after(place, part0[0]), pieces[1])
    got1 = send_first(part1)
    value0 = onward(part0, after(got0, part1[0], *near[2]))
    got0 = send_second(value0, got0)
    part2 = gram_parts(after(place, value0), pieces[2])
    got2 = send_first(part2)
    value1 = onward(part1, after(got1, part2[0]))
    got1 = send_second(value1, got1)
    rows0 = owned(part0, after(got0, value1))
    terms = [send_rows(rows0)]
    kept_part, given_part, note = direction_of(after(place, rows0, *got2), adagrad_sq, pieces, root_pieces)
    given_part = swap_cores(given_part)
    value2 = onward(part2, after(got2, note))
    got2 = send_second(value2, got2)
    rows1 = owned(part1, after(got1, value2), note)
    terms.append(send_rows(rows1))
    terms[0] = after(terms[0], rows1)
    sums = terms[1][:, -TAIL : 3 - TAIL].astype(F32)
    sums = (sums[:, 1] + sums[:, 2] / LOW) * jnp.exp2(sums[:, 0])
    sums = jnp.sum(sums.reshape(experts, NZ, slab), axis=1)
    rows2 = owned(part2, after(got2, rows1))
    terms.append(send_rows(after(rows2, terms[1])))
    sums = sums + step_x(sums, 1) + step_x(sums, -1) + step_x(sums, 2)
    sums = sums + step_y(sums, 1) + step_y(sums, -1) + step_y(sums, 2)
    count = experts * blocks
    sums = jnp.sum(sums[:, :count], axis=0).reshape(experts, blocks), sums[:, count : count + blocks]
    statistic = jnp.stack([add_rows(term) for term in terms], axis=1)
    graft_scale = jnp.sqrt(sums[0]) / jnp.sqrt(sums[1] + 1e-06)
    step = scaled_step(place, graft_scale, kept_part, given_part)
    return (statistic, step.transpose(0, 2, 1, 3))


def solution(mesh):
    placed = (P(None, "fsdp", None, "tp"), P(None, "fsdp", None, "tp"), P(None, None, "fsdp", "tp"))
    return jax.shard_map(
        on_device,
        mesh=mesh,
        in_specs=placed,
        out_specs=(P(None, None, "fsdp", "tp"), P(None, "fsdp", None, "tp")),
        check_vma=False,
    )
```

```python
import functools
import jax
import jax.numpy as jnp
from jax import lax
from jax.experimental import pallas as pl
from jax.experimental.pallas import tpu as pltpu
from jax.sharding import PartitionSpec as P

EPS = 1e-08
NZ, NX, NY, NC = 8, 4, 4, 2
AXES = ("fsdp", "tp")
F32 = jnp.float32
F16 = jnp.float16
TAIL = 8
LARGEST = 14.0
LOW = 256.0


def turn(c):
    return 1 - 2 * c


def device(z, x, y, c):
    return ((z * NX + x) * NY + y) * NC + c


EVERY = [(z, x, y, c) for z in range(NZ) for x in range(NX) for y in range(NY) for c in range(NC)]


def step_x(value, by):
    pairs = [(device(z, x, y, c), device(z, (x + by * turn(c)) % NX, y, c)) for z, x, y, c in EVERY]
    return lax.ppermute(value, AXES, pairs)


def step_y(value, by):
    pairs = [(y * NC + c, (y + by * turn(c)) % NY * NC + c) for y in range(NY) for c in range(NC)]
    return lax.ppermute(value, "tp", pairs)


def shift_x(value, by):
    pairs = [(z * NX + x, z * NX + (x + by) % NX) for z in range(NZ) for x in range(NX)]
    return lax.ppermute(value, "fsdp", pairs)


def swap_cores(value):
    return lax.ppermute(value, "tp", [(i, i ^ 1) for i in range(NY * NC)])


GROUPS_CZ = [
    [device(z, x, y, c) for c in range(NC) for z in range(NZ)] for x in range(NX) for y in range(NY)
]
GROUPS_Y = [[device(z, x, y, c) for y in range(NY) for c in range(NC)] for z in range(NZ) for x in range(NX)]
GROUPS_Z = [[device(z, x, y, c) for z in range(NZ)] for x in range(NX) for y in range(NY) for c in range(NC)]
RING_Z = [[z * NX + x for z in range(NZ)] for x in range(NX)]


def swap_cores(value):
    return lax.ppermute(value, "tp", [(i, i ^ 1) for i in range(NY * NC)])


GROUPS_CZ = [
    [device(z, x, y, c) for c in range(NC) for z in range(NZ)] for x in range(NX) for y in range(NY)
]
GROUPS_Y = [[device(z, x, y, c) for y in range(NY) for c in range(NC)] for z in range(NZ) for x in range(NX)]
GROUPS_Z = [[device(z, x, y, c) for z in range(NZ)] for x in range(NX) for y in range(NY) for c in range(NC)]
RING_Z = [[z * NX + x for z in range(NZ)] for x in range(NX)]


SWAPS = (
    (0, 2, 0, 0),
    (0, 1, 0, 0),
    (0, 0, 2, 0),
    (0, 0, 1, 0),
)


def swap(value, dz, dx, dy, dc):
    pairs = [(device(z, x, y, c), device(z ^ dz, x ^ dx, y ^ dy, c ^ dc)) for z, x, y, c in EVERY]
    return lax.ppermute(value, AXES, pairs)


def spread(value, groups):
    copies = jnp.broadcast_to(value[None], (len(groups[0]),) + value.shape)
    return lax.all_to_all(copies, AXES, 0, 0, axis_index_groups=groups)


def after(value, *others):
    return lax.optimization_barrier((value,) + others)[0]


def contract_rows(a, b):
    return lax.dot_general(a, b, (((0,), (0,)), ((), ())), preferred_element_type=F32)


def gram_kernel(place, own, behind, beyond, ahead, cols, *refs):
    outs, terms = refs[:NX], refs[NX]
    xi, yi, sense = place[0], place[1], 1 - 2 * place[2]
    rows = terms.shape[2]
    top = None
    for piece, dy in ((own, 0), (behind, -1), (beyond, -2), (ahead, 1)):
        part = lax.dot_general(
            piece[...], cols[...], (((0,), (0,)), ((), ())), preferred_element_type=F32
        )
        large = jnp.max(jnp.abs(part), axis=0, keepdims=True)
        top = large if top is None else jnp.maximum(top, large)
        y = lax.rem(yi + sense * dy + NY, NY)
        for i in range(2):
            for x in range(NX):
                first = (i * NX + x) * rows
                to = lax.rem((x - xi) * sense + NX, NX)
                terms[to, 2 * y + i] = part[first : first + rows]
    code = jnp.ceil(jnp.log2(jnp.clip(top, 2.0**-100, 2.0**100)))
    factor = jnp.exp2(LARGEST - code)
    tail = jnp.broadcast_to(code, (TAIL, code.shape[1]))
    for to, out in enumerate(outs):
        for z in range(NZ):
            out[0, z, :rows] = terms[to, z] * factor
            out[0, z, rows:] = tail


def gram_parts(place, pieces):
    local_rows, wide = pieces[0].shape
    rows, cols = wide * NY // (NX * NZ), wide // NC
    whole = [pl.BlockSpec(piece.shape, lambda i, s: (0, 0)) for piece in pieces]
    shape = (NC, NZ, rows + TAIL, cols)
    return pl.pallas_call(
        gram_kernel,
        grid_spec=pltpu.PrefetchScalarGridSpec(
            num_scalar_prefetch=1,
            grid=(NC,),
            in_specs=whole + [pl.BlockSpec((local_rows, cols), lambda i, s: (0, i))],
            out_specs=[pl.BlockSpec((1,) + shape[1:], lambda i, s: (i, 0, 0, 0))] * NX,
            scratch_shapes=[pltpu.VMEM((NX, NZ, rows, cols), F32)],
        ),
        out_shape=[jax.ShapeDtypeStruct(shape, F32)] * NX,
        compiler_params=pltpu.CompilerParams(vmem_limit_bytes=32 << 20),
        cost_estimate=pl.CostEstimate(
            flops=2 * local_rows * wide * wide * NY,
            bytes_accessed=2 * local_rows * wide * NY + 4 * wide * wide * NY,
            transcendentals=0,
        ),
    )(place, *pieces, pieces[0])


def power(code):
    return jnp.left_shift(1, 30 + jnp.maximum(code, -30.0).astype(jnp.int32)).astype(F32) * 2.0**-30


def add_scaled(*terms, note=None):
    codes = [term[:, :1, -1:].astype(F32) for term in terms]
    code = functools.reduce(jnp.maximum, codes) + (len(terms) - 1)
    total = sum(term.astype(F32) * power(own - code) for term, own in zip(terms, codes))
    row = lax.broadcasted_iota(jnp.int32, total.shape, 2)
    rest = code if note is None else jnp.where(row == total.shape[2] - 1, code, note)
    return jnp.where(row >= total.shape[2] - TAIL, rest, total).astype(F16)


def direction_kernel(blocks, place, adagrad, *refs):
    pieces, roots = refs[: NY * blocks], refs[NY * blocks]
    mine, theirs, note, whole, root, sems = refs[NY * blocks + 1 :]
    xi, yi, ci = place[0], place[1], place[2]
    sense = 1 - 2 * ci
    wide, slab = root.shape[-1], mine.shape[-1]
    copies = []
    for j in range(blocks):
        group = [(roots.at[:, dx, j], root.at[j, :, lax.rem(xi + dx, NX)]) for dx in range(NX)]
        for k, dy in enumerate((0, -1, -2, 1)):
            start = pl.multiple_of(lax.rem(yi + sense * dy + NY, NY) * wide, wide)
            group.append((pieces[NY * j + k], whole.at[j, :, pl.ds(start, wide)]))
        copies.append(
            [pltpu.make_async_copy(a, b, sems.at[j, i]) for i, (a, b) in enumerate(group)]
        )
    for copy in copies[0]:
        copy.start()
    sums = [adagrad[e, j] for e in range(NC) for j in range(blocks)]
    for j in range(blocks):
        if j + 1 < blocks:
            for copy in copies[j + 1]:
                copy.start()
        for copy in copies[j]:
            copy.wait()
        value = jnp.dot(
            whole[j], root[j].reshape(NY * wide, wide), preferred_element_type=F32
        )
        first, second = value[:, :slab], value[:, slab:]
        mine[j] = jnp.where(ci == 0, first, second)
        theirs[j] = jnp.where(ci == 0, second, first)
        sums.append(jnp.sum(value * value))
    lane = lax.broadcasted_iota(jnp.int32, (1, note.shape[1]), 1)
    line = jnp.zeros(lane.shape, F32)
    for i, value in enumerate(sums):
        line = jnp.where(lane == i, value, line)
    code = jnp.ceil(jnp.log2(jnp.clip(line, 2.0**-100, 2.0**100)))
    line = line * jnp.exp2(-code)
    high = line.astype(jnp.bfloat16).astype(F32)
    rows = note.shape[0] - TAIL
    note[...] = jnp.zeros(note.shape, F32)
    for i, value in enumerate((code, high, (line - high) * LOW)):
        note[rows + i : rows + i + 1] = value


def direction_of(place, adagrad_sq, pieces, roots):
    blocks = len(pieces)
    local_rows, wide = pieces[0][0].shape
    rows, slab = roots.shape[3], wide // NC
    result = jax.ShapeDtypeStruct((blocks, local_rows, slab), F32)
    vmem = pl.BlockSpec(memory_space=pltpu.VMEM)
    return pl.pallas_call(
        functools.partial(direction_kernel, blocks),
        in_specs=[pl.BlockSpec(memory_space=pltpu.SMEM)] * 2
        + [pl.BlockSpec(memory_space=pltpu.HBM)] * (NY * blocks + 1),
        out_specs=[vmem, vmem, vmem],
        out_shape=[result, result, jax.ShapeDtypeStruct((rows + TAIL, slab), F32)],
        scratch_shapes=[
            pltpu.VMEM((blocks, local_rows, NY * wide), jnp.bfloat16),
            pltpu.VMEM((blocks, NZ, NX, rows, wide), jnp.bfloat16),
            pltpu.SemaphoreType.DMA((blocks, NX + NY)),
        ],
        compiler_params=pltpu.CompilerParams(vmem_limit_bytes=60 << 20),
        cost_estimate=pl.CostEstimate(
            flops=2 * blocks * local_rows * wide * wide * NY,
            bytes_accessed=2 * blocks * (local_rows + wide) * wide * NY + 4 * blocks * local_rows * wide,
            transcendentals=0,
        ),
    )(place, adagrad_sq, *[piece for group in pieces for piece in group], roots)


def step_kernel(place, scale, kept, given, out):
    core, j = place[2], pl.program_id(0)
    out[core, 0] = kept[0] * scale[core, j]
    out[1 - core, 0] = given[0] * scale[1 - core, j]


def scaled_step(place, scale, kept, given):
    blocks, local_rows, slab = kept.shape
    return pl.pallas_call(
        step_kernel,
        grid=(blocks,),
        in_specs=[pl.BlockSpec(memory_space=pltpu.SMEM)] * 2
        + [pl.BlockSpec((1, local_rows, slab), lambda j: (j, 0, 0))] * 2,
        out_specs=pl.BlockSpec((NC, 1, local_rows, slab), lambda j: (0, j, 0, 0)),
        out_shape=jax.ShapeDtypeStruct((NC, blocks, local_rows, slab), F32),
        compiler_params=pltpu.CompilerParams(vmem_limit_bytes=32 << 20),
        cost_estimate=pl.CostEstimate(
            flops=2 * blocks * local_rows * slab,
            bytes_accessed=16 * blocks * local_rows * slab,
            transcendentals=0,
        ),
    )(place, scale, kept, given)


def on_device(grads, accum, roots):
    experts, local_rows, blocks, slab = grads.shape
    fsdp, tp = lax.axis_index("fsdp"), lax.axis_index("tp")
    core = lax.rem(tp, NC)
    first_core = core == 0
    place = jnp.stack([lax.rem(fsdp, NX), tp // NC, core]).astype(jnp.int32)
    rows_total = local_rows * lax.axis_size("fsdp")
    mine = grads.transpose(0, 2, 1, 3)

    def pick(pair):
        return jnp.where(first_core, pair[0], pair[1]), jnp.where(first_core, pair[1], pair[0])

    def by_core(kept, given):
        return jnp.concatenate(pick((kept, given)), axis=-1)

    (kept_grads, other_grads), (kept_roots, other_roots) = pick(mine), pick(roots)
    given = swap_cores(jnp.concatenate([other_grads, other_roots], axis=1))
    given_grads, given_roots = given[:, :local_rows], given[:, local_rows:]

    chip = [by_core(kept_grads[j], given_grads[j]) for j in range(blocks)]
    root = by_core(kept_roots, given_roots)
    chip[0], chip[1], chip[2], root = lax.optimization_barrier((*chip, root))

    def send_near(own):
        return step_y(own, 1), step_y(own, -1)

    near = [send_near(chip[0])]
    root = [root, shift_x(root, -1), shift_x(root, 2), shift_x(root, 1)]
    root = jnp.stack(lax.optimization_barrier((*root, *near[0]))[:NX])
    root_pieces = lax.all_gather(root, "fsdp", axis=0, axis_index_groups=RING_Z)

    near.append(send_near(after(chip[1], *near[0])))
    gradient = mine.astype(F32)
    adagrad = gradient / (jnp.sqrt(accum.transpose(0, 2, 1, 3) + gradient * gradient) + EPS)
    adagrad_sq = jnp.sum(adagrad * adagrad, axis=(2, 3))

    def collect(j, *wait):
        behind = after(near[j][0], *wait) if wait else near[j][0]
        return chip[j], near[j][0], step_y(behind, 1), near[j][1]

    def send_first(part):
        return step_x(part[2].astype(F16), 1), step_x(part[3].astype(F16), -1)

    def onward(part, arrived):
        return add_scaled(part[1], arrived[0])

    def send_second(value, arrived):
        return step_x(value, 1), arrived[1]

    def owned(part, arrived, note=None):
        return add_scaled(part[0], *arrived, note=note)

    def send_rows(summed):
        summed = summed.reshape((NC * NZ,) + summed.shape[2:])
        return lax.all_to_all(summed, AXES, 0, 0, axis_index_groups=GROUPS_CZ)

    def add_rows(term):
        term = term.reshape((experts, NZ) + term.shape[1:])
        factor = jnp.exp2(term[..., -1:, :].astype(F32) - LARGEST)
        return (jnp.sum(term.astype(F32) * factor, axis=1) / rows_total)[..., :-TAIL, :]

    pieces = [collect(0), collect(1)]
    near.append(send_near(after(chip[2], pieces[1][2])))
    pieces.append(collect(2))
    part0 = gram_parts(after(place, adagrad_sq, *near[1]), pieces[0])
    got0 = send_first(part0)
    part1 = gram_parts(after(place, part0[0]), pieces[1])
    got1 = send_first(part1)
    value0 = onward(part0, after(got0, part1[0], *near[2]))
    got0 = send_second(value0, got0)
    part2 = gram_parts(after(place, value0), pieces[2])
    got2 = send_first(part2)
    value1 = onward(part1, after(got1, part2[0]))
    got1 = send_second(value1, got1)
    rows0 = owned(part0, after(got0, value1))
    terms = [send_rows(rows0)]
    kept_part, given_part, note = direction_of(after(place, rows0, *got2), adagrad_sq, pieces, root_pieces)
    given_part = swap_cores(given_part)
    value2 = onward(part2, after(got2, note))
    got2 = send_second(value2, got2)
    rows1 = owned(part1, after(got1, value2), note)
    terms.append(send_rows(rows1))
    terms[0] = after(terms[0], rows1)
    sums = terms[1][:, -TAIL : 3 - TAIL].astype(F32)
    sums = (sums[:, 1] + sums[:, 2] / LOW) * jnp.exp2(sums[:, 0])
    sums = jnp.sum(sums.reshape(experts, NZ, slab), axis=1)
    rows2 = owned(part2, after(got2, rows1))
    terms.append(send_rows(after(rows2, terms[1])))
    sums = sums + step_x(sums, 1)
    sums = sums + step_x(sums, 2)
    sums = sums + step_y(sums, 1) + step_y(sums, -1) + step_y(sums, 2)
    count = experts * blocks
    sums = jnp.sum(sums[:, :count], axis=0).reshape(experts, blocks), sums[:, count : count + blocks]
    statistic = jnp.stack([add_rows(term) for term in terms], axis=1)
    graft_scale = jnp.sqrt(sums[0]) / jnp.sqrt(sums[1] + 1e-06)
    step = scaled_step(place, graft_scale, kept_part, given_part)
    return (statistic, step.transpose(0, 2, 1, 3))


def solution(mesh):
    placed = (P(None, "fsdp", None, "tp"), P(None, "fsdp", None, "tp"), P(None, None, "fsdp", "tp"))
    return jax.shard_map(
        on_device,
        mesh=mesh,
        in_specs=placed,
        out_specs=(P(None, None, "fsdp", "tp"), P(None, "fsdp", None, "tp")),
        check_vma=False,
    )
```
